32 devices in a mesh: leaf: 4 (over y, x), sub: 8 (over z, core).
Axes of the slice: x: 2, y: 2, z: 4, core: 2. Of those that a mesh axis runs over, the one named last changes fastest.
Arguments:
- points: float32 [1536, 3, 256], P(('leaf', 'sub')), may hold values from -1 to 1
- amplitude: float32 [1536, 256], P(('leaf', 'sub')), may hold values from 0.5 to 2
- vectors: float32 [1536, 8, 256], P(('leaf', 'sub')), may hold values from -6 to 6
- basis: float32 [1536, 256, 64], P(('leaf', 'sub')), may hold values from -0.375 to 0.375
- transfer: float32 [1536, 64, 64], P(('leaf', 'sub')), may hold values from -0.25 to 0.25
- couplings: float32 [1536, 16, 64, 64], P(('leaf', 'sub')), may hold values from -0.1875 to 0.1875
- coarse_couplings: float32 [192, 32, 64, 64], P(('leaf', 'sub')), may hold values from -0.125 to 0.125
- near_list: int32 [1536, 16], P(('leaf', 'sub')), may hold values from -1 to 1535, as said below
- far_list: int32 [1536, 16], P(('leaf', 'sub')), may hold values from -1 to 1535, as said below
- coarse_list: int32 [192, 32], P(('leaf', 'sub')), may hold values from -1 to 191, as said below
Outputs:
- product: float32 [1536, 8, 256], P(('leaf', 'sub'))
The draws below stay inside these ranges and needn't reach their ends.
Inputs may be any that keep to these rules, and one draw needn't show every extreme that they name: `near_list`: slot 0 of leaf i is i itself; the other filled slots name distinct leaves within 48 positions of i in octree order; some leaves fill all 16 slots. `far_list`: filled slots name distinct leaves within 48 positions of i, none of them in leaf i's near list nor i itself; some leaves fill all 16 slots. `coarse_list`: filled slots name distinct parents other than p itself; filled slots come first, then -1; some parents fill all 32 slots.
All inputs are finite; a program needn't handle non-finite values.
Results may differ from the reference program's by a relative error of at most 0.0003.
Values sent between devices are 32-bit elements; how exact they have to be, the bound alone decides.
A program may use at most 128 MiB of HBM per device.

```python
import math
import jax
import jax.numpy as jnp
from jax import lax

LEAF = 256
BASIS_RANK = 64
VECTOR_COUNT = 8
NEAR = 16
FAR = 16
FAR2 = 32
L_DEV = 48
TOTAL_LEAVES = 1536
PARENT_BOXES = 192


def offset_table(key):
    cand = jnp.concatenate([jnp.arange(-L_DEV, 0), jnp.arange(1, L_DEV + 1)]).astype(jnp.int32)
    keys = jax.random.split(key, TOTAL_LEAVES)
    return jax.vmap(lambda one: jax.random.permutation(one, cand))(keys)


def fill_list(key, offsets, width):
    rows = jnp.arange(TOTAL_LEAVES, dtype=jnp.int32)[:, None]
    target = rows + offsets
    inside = (target >= 0) & (target < TOTAL_LEAVES)
    counts = jax.random.randint(key, (TOTAL_LEAVES, 1), width // 2, width + 1)
    counts = jnp.where(rows % 5 == 2, width, counts)
    column = jnp.arange(width, dtype=jnp.int32)[None, :]
    keep = inside & (column < counts)
    return jnp.where(keep, target, -1).astype(jnp.int32)


def draw_near_list(key, part):
    offsets = offset_table(key)
    key = jax.random.fold_in(key, 1)
    rows = jnp.arange(TOTAL_LEAVES, dtype=jnp.int32)[:, None]
    others = fill_list(key, offsets[:, :NEAR - 1], NEAR - 1)
    return jnp.concatenate([rows, others], axis=1).astype(jnp.int32)


def draw_far_list(key, part):
    offsets = offset_table(key)
    key = jax.random.fold_in(key, 2)
    return fill_list(key, offsets[:, NEAR - 1:NEAR - 1 + FAR], FAR)


def draw_coarse_list(key, part):
    key = jax.random.fold_in(key, 3)
    perm_key, count_key = jax.random.split(key)
    keys = jax.random.split(perm_key, PARENT_BOXES)
    base = jnp.arange(PARENT_BOXES - 1, dtype=jnp.int32)
    perms = jax.vmap(lambda one: jax.random.permutation(one, base))(keys)[:, :FAR2]
    rows = jnp.arange(PARENT_BOXES, dtype=jnp.int32)[:, None]
    target = (rows + 1 + perms) % PARENT_BOXES
    counts = jax.random.randint(count_key, (PARENT_BOXES, 1), FAR2 // 2, FAR2 + 1)
    counts = jnp.where(rows % 5 == 2, FAR2, counts)
    column = jnp.arange(FAR2, dtype=jnp.int32)[None, :]
    return jnp.where(column < counts, target, -1).astype(jnp.int32)


def block_scale(key, shape, cuts, least, largest):
    def one(axis_at, shards_of):
        steps = jax.random.uniform(jax.random.fold_in(jax.random.fold_in(key, 6), axis_at), (shards_of,), jnp.float32, least / len(cuts), largest / len(cuts))
        return jnp.repeat(jnp.exp(steps), shape[axis_at] // shards_of).reshape((-1,) + (1,) * (len(shape) - axis_at - 1))

    gain = one(*cuts[0])
    for cut in cuts[1:]:
        gain = gain * one(*cut)
    return gain


def gaussian(rng, dims, spread, reach, pieces=(), kind=jnp.bfloat16):
    values = jax.random.normal(rng, dims, jnp.float32) * spread
    if len(pieces) > 0:
        values = block_scale(rng, dims, pieces, -0.22, 0.18) * values
    return jnp.clip(values, min=-reach, max=reach).astype(kind)


def setup_inputs(seed: int = 0) -> dict:
    key_list = jax.random.split(jax.random.key(seed), 11)
    return {
        "points": jnp.clip(jax.random.uniform(key_list[0], (TOTAL_LEAVES, 3, LEAF), jnp.float32, -1.0, 1.0) * block_scale(key_list[0], (TOTAL_LEAVES, 3, LEAF), ((0, 32),), -0.4, 0.0), -1.0, 1.0),
        "amplitude": jnp.clip(jnp.exp(math.log(2.0) - 1.3862944 * jax.random.uniform(key_list[1], (TOTAL_LEAVES, LEAF), jnp.float32) ** block_scale(key_list[1], (TOTAL_LEAVES, LEAF), ((0, 32),), -0.2, 0.2)), 0.5, 2.0),
        "vectors": gaussian(key_list[2], (TOTAL_LEAVES, VECTOR_COUNT, LEAF), 1.0, 6.0, ((0, 32),), jnp.float32),
        "basis": gaussian(key_list[3], (TOTAL_LEAVES, LEAF, BASIS_RANK), LEAF ** -0.5, 0.375, ((0, 32),), jnp.float32),
        "transfer": gaussian(key_list[4], (TOTAL_LEAVES, BASIS_RANK, BASIS_RANK), (8 * BASIS_RANK) ** -0.5, 0.25, ((0, 32),), jnp.float32),
        "couplings": gaussian(key_list[5], (TOTAL_LEAVES, FAR, BASIS_RANK, BASIS_RANK), (BASIS_RANK * FAR) ** -0.5, 0.1875, ((0, 32),), jnp.float32),
        "coarse_couplings": gaussian(key_list[6], (PARENT_BOXES, FAR2, BASIS_RANK, BASIS_RANK), (BASIS_RANK * FAR2) ** -0.5, 0.125, ((0, 32),), jnp.float32),
        "near_list": draw_near_list(jax.random.fold_in(key_list[10], 71), 0),
        "far_list": draw_far_list(jax.random.fold_in(key_list[10], 71), 0),
        "coarse_list": draw_coarse_list(jax.random.fold_in(key_list[10], 71), 0),
    }


ELL2 = 0.25
HIGHEST_LEVEL = lax.Precision.HIGHEST


def reference(points, amplitude, vectors, basis, transfer, couplings, coarse_couplings, near_list, far_list, coarse_list):
    near_gain = 4.0 * (LEAF * NEAR) ** -0.5

    def near_one(index):
        slots = near_list[index]
        valid = slots >= 0
        safe = jnp.where(valid, slots, 0).astype(jnp.int32)
        own = points[index]
        other = points[safe]
        dist = jnp.zeros((NEAR, LEAF, LEAF), jnp.float32)
        for comp in range(3):
            delta = own[comp][None, :, None] - other[:, comp][:, None, :]
            dist = dist + delta * delta
        kern = jnp.exp(-dist / (2.0 * ELL2)) * amplitude[index][None, :, None] * amplitude[safe][:, None, :] * valid.astype(jnp.float32)[:, None, None]
        return near_gain * jnp.einsum('nij,nvj->vi', kern, vectors[safe], precision=HIGHEST_LEVEL)

    near = lax.map(near_one, jnp.arange(TOTAL_LEAVES, dtype=jnp.int32))
    leaf_coefficients = jnp.einsum('lpr,lvp->lrv', basis, vectors, precision=HIGHEST_LEVEL)
    fvalid = far_list >= 0
    fsafe = jnp.where(fvalid, far_list, 0).astype(jnp.int32)
    got = leaf_coefficients[fsafe] * fvalid.astype(jnp.float32)[:, :, None, None]
    leaf_field = jnp.einsum('lkrs,lksv->lrv', couplings, got, precision=HIGHEST_LEVEL)
    transposed_fourth = transfer.reshape(PARENT_BOXES, 8, BASIS_RANK, BASIS_RANK)
    parent_coefficients = jnp.einsum('xhjk,xhji->xki', transposed_fourth, leaf_coefficients.reshape(PARENT_BOXES, 8, BASIS_RANK, VECTOR_COUNT), precision=HIGHEST_LEVEL)
    cvalid = coarse_list >= 0
    csafe = jnp.where(cvalid, coarse_list, 0).astype(jnp.int32)
    cgot = parent_coefficients[csafe] * cvalid.astype(jnp.float32)[:, :, None, None]
    parent_level_field = jnp.einsum('pkst,pktv->psv', coarse_couplings, cgot, precision=HIGHEST_LEVEL)
    downward_pass = jnp.einsum('oxzf,ofk->oxzk', transposed_fourth, parent_level_field, precision=HIGHEST_LEVEL).reshape(TOTAL_LEAVES, BASIS_RANK, VECTOR_COUNT)
    field = leaf_field + downward_pass
    far = jnp.einsum('lpr,lrv->lvp', basis, field, precision=HIGHEST_LEVEL)
    return near + far
```

```python
import math

import jax
import jax.numpy as jnp
from jax import lax
from jax.experimental import pallas as pl
from jax.experimental.pallas import tpu as pltpu
from jax.sharding import PartitionSpec as P

LEAF = 256
NEAR = 16
ELL2 = 0.25
AXES = ("leaf", "sub")
CHILDREN = 8
FEATURES = 32
VMEM_BYTES = 56 * 1024 * 1024
f32 = jnp.float32
bf16 = jnp.bfloat16


def halo(cells):
    ends = lax.axis_size(AXES) - 1
    before = lax.ppermute(cells, AXES, [(i, i + 1) for i in range(ends)])
    after = lax.ppermute(cells, AXES, [(i + 1, i) for i in range(ends)])
    return before, after


def three(x):
    high = x.astype(bf16).astype(f32)
    rest = x - high
    mid = rest.astype(bf16).astype(f32)
    return high, mid, rest - mid


def split(x):
    high = x.astype(bf16)
    return high, (x - high.astype(f32)).astype(bf16)


def stacked_rows(x):
    high = x.astype(bf16).astype(f32)
    return jnp.concatenate([high, x - high], axis=0).astype(bf16)


def dot(a, b):
    return jnp.dot(a, b, preferred_element_type=f32)


def dot_t(a, b):
    return lax.dot_general(a, b, (((1,), (1,)), ((), ())), preferred_element_type=f32)


def folded(x):
    half = x.shape[0] // 2
    return x[:half] + x[half:]


def up_kernel(vectors, basis, transfer, coefs, parents):
    total = jnp.zeros((16, transfer.shape[2]), f32)
    for q in range(CHILDREN):
        high, low = split(basis[q])
        rows = stacked_rows(vectors[q])
        one = folded(dot_t(rows, high) + dot_t(rows, low))
        coefs[q] = one
        rows = stacked_rows(one)
        high, low = split(transfer[q])
        total = total + dot(rows, high) + dot(rows, low)
    parents[0] = folded(total)


def pieces(points, at):
    scale = math.sqrt(math.log2(math.e) / ELL2)
    rows = [points[c, pl.ds(at, 1), :] for c in range(3)]
    x = jnp.concatenate(rows, axis=0) * scale
    norm = -0.5 * jnp.sum(x * x, axis=0, keepdims=True)
    ones = jnp.ones((3, x.shape[1]), f32)
    rest = jnp.zeros((FEATURES - 24, x.shape[1]), f32)
    return three(x), three(norm), ones, rest


def own_features(points, at):
    (h, m, l), norm, ones, rest = pieces(points, at)
    return jnp.concatenate([h, m, h, l, h, m, *norm, ones, rest], axis=0).astype(bf16)


def other_features(points, at):
    (h, m, l), norm, ones, rest = pieces(points, at)
    rows = jnp.concatenate([h, h, m, h, l, m, ones, *norm, rest], axis=0)
    return jnp.transpose(rows).astype(bf16)


def near_kernel(
    slots,
    points_before,
    points_own,
    points_after,
    vectors_before,
    vectors_own,
    vectors_after,
    out,
    others,
    values,
    filled,
):
    blank = others.shape[0] - 1
    base = pl.program_id(0) * CHILDREN
    ldev = blank // 3

    @pl.when(pl.program_id(0) == 0)
    def _():
        sides = (
            (points_before, vectors_before),
            (points_own, vectors_own),
            (points_after, vectors_after),
        )

        def prepare(at, carry):
            for side, (points, vectors) in enumerate(sides):
                where = side * ldev + at
                others[where] = other_features(points, at)
                values[where] = stacked_rows(vectors[at] * points[3, pl.ds(at, 1), :])
            return carry

        lax.fori_loop(0, ldev, prepare, 0)
        others[blank] = jnp.zeros(others.shape[1:], bf16)
        values[blank] = jnp.zeros(values.shape[1:], bf16)

    gain = 4.0 * (LEAF * NEAR) ** (-0.5)
    width = slots.shape[1]

    def leaf(q, carry):
        count = jnp.int32(0)
        for n in range(width):
            j = slots[base + q, n]
            filled[count] = j
            count = count + jnp.where(j < blank, 1, 0)
        for n in range(3):
            filled[count + n] = blank
        mine = own_features(points_own, base + q)

        def some(first, many, total):
            for u in range(many):
                j = filled[first + u]
                kern = jnp.exp2(dot(others[j], mine))
                high, low = split(kern)
                rows = values[j]
                total = total + dot(rows, high) + dot(rows, low)
            return total

        total = jnp.zeros((16, out.shape[2]), f32)
        fours = (count + 1) // 4
        total = lax.fori_loop(0, fours, lambda g, t: some(4 * g, 4, t), total)
        twos = jnp.where(count > 4 * fours, 1, 0)
        total = lax.fori_loop(0, twos, lambda g, t: some(4 * fours, 2, t), total)
        out[q] = folded(total) * (gain * points_own[3, pl.ds(base + q, 1), :])
        return carry

    lax.fori_loop(0, CHILDREN, leaf, 0)


def coupled(index, slots, table, matrix):
    rank = table.shape[2]
    total = jnp.zeros((64, 4 * rank), f32)
    for g in range(slots.shape[1] // 4):
        rows = jnp.concatenate([table[slots[index, 4 * g + u]] for u in range(4)], axis=0)
        high, low = split(matrix(4 * g))
        total = total + dot_t(rows, high) + dot_t(rows, low)
    blocks = [total[16 * u : 16 * u + 16, rank * u : rank * u + rank] for u in range(4)]
    return folded(blocks[0] + blocks[1] + blocks[2] + blocks[3])


def far_kernel(
    far_slots,
    coarse_slots,
    coefs_before,
    coefs_own,
    coefs_after,
    every,
    couplings,
    coarse,
    transfer,
    basis,
    near,
    out,
    coefs,
    parents,
):
    rank = transfer.shape[2]
    step = pl.program_id(0)
    ldev = coefs_own.shape[0]

    @pl.when(step == 0)
    def _():
        def prepare(at, carry):
            coefs[at] = stacked_rows(coefs_before[at])
            coefs[ldev + at] = stacked_rows(coefs_own[at])
            coefs[2 * ldev + at] = stacked_rows(coefs_after[at])
            return carry

        def prepare_parent(at, carry):
            parents[at] = stacked_rows(every[at])
            return carry

        lax.fori_loop(0, ldev, prepare, 0, unroll=2)
        lax.fori_loop(0, every.shape[0], prepare_parent, 0, unroll=4)
        coefs[3 * ldev] = jnp.zeros(coefs.shape[1:], bf16)
        parents[every.shape[0]] = jnp.zeros(parents.shape[1:], bf16)

    field = coupled(
        step, coarse_slots, parents, lambda k: coarse[0, k : k + 4].reshape(4 * rank, rank)
    )
    above = stacked_rows(field)

    def leaf(q, carry):
        field = coupled(
            step * CHILDREN + q,
            far_slots,
            coefs,
            lambda k: couplings[q, k : k + 4].reshape(4 * rank, rank),
        )
        high, low = split(transfer[q])
        field = field + folded(dot_t(above, high) + dot_t(above, low))
        rows = stacked_rows(field)
        high, low = split(basis[q])
        out[q] = near[q] + folded(dot(rows, high) + dot(rows, low))
        return carry

    lax.fori_loop(0, CHILDREN, leaf, 0)


def whole(x):
    return pl.BlockSpec(x.shape, lambda i: (0,) * x.ndim)


def part(x, rows):
    return pl.BlockSpec((rows,) + x.shape[1:], lambda i: (i,) + (0,) * (x.ndim - 1))


def scalars():
    return pl.BlockSpec(memory_space=pltpu.SMEM)


def params():
    return pltpu.CompilerParams(vmem_limit_bytes=VMEM_BYTES)


def on_device(
    points,
    amplitude,
    vectors,
    basis,
    transfer,
    couplings,
    coarse_couplings,
    near_list,
    far_list,
    coarse_list,
):
    ldev, _, leaf_size = points.shape
    rank = transfer.shape[2]
    count = vectors.shape[1]
    nparents = ldev // CHILDREN
    offset = lax.axis_index(AXES) * ldev - ldev
    blank = 3 * ldev

    basis = basis.swapaxes(1, 2)
    sites = jnp.concatenate([points.swapaxes(0, 1), amplitude[None]], axis=0)
    points_before, points_after = halo(sites)
    vectors_before, vectors_after = halo(vectors)

    coefs, parents = pl.pallas_call(
        up_kernel,
        grid=(nparents,),
        out_shape=(
            jax.ShapeDtypeStruct((ldev, count, rank), f32),
            jax.ShapeDtypeStruct((nparents, count, rank), f32),
        ),
        in_specs=[part(vectors, CHILDREN), part(basis, CHILDREN), part(transfer, CHILDREN)],
        out_specs=(
            pl.BlockSpec((CHILDREN, count, rank), lambda i: (i, 0, 0)),
            pl.BlockSpec((1, count, rank), lambda i: (i, 0, 0)),
        ),
        compiler_params=params(),
        cost_estimate=pl.CostEstimate(
            flops=8 * ldev * leaf_size * rank * 16,
            bytes_accessed=12 * ldev * leaf_size * rank,
            transcendentals=0,
        ),
        name="upward",
    )(vectors, basis, transfer)

    every = lax.all_gather(parents, AXES, axis=0, tiled=True)
    coefs_before, coefs_after = halo(coefs)

    near_slots = jnp.where(near_list >= 0, near_list - offset, blank)
    far_slots = jnp.where(far_list >= 0, far_list - offset, blank)
    coarse_slots = jnp.where(coarse_list >= 0, coarse_list, every.shape[0])

    pairs = ldev * near_list.shape[1]
    near = pl.pallas_call(
        near_kernel,
        grid=(nparents,),
        out_shape=jax.ShapeDtypeStruct((ldev, count, leaf_size), f32),
        in_specs=[scalars()] + [whole(sites)] * 3 + [whole(vectors)] * 3,
        out_specs=pl.BlockSpec((CHILDREN, count, leaf_size), lambda i: (i, 0, 0)),
        scratch_shapes=[
            pltpu.VMEM((blank + 1, leaf_size, FEATURES), bf16),
            pltpu.VMEM((blank + 1, 2 * count, leaf_size), bf16),
            pltpu.SMEM((near_list.shape[1] + 8,), jnp.int32),
        ],
        compiler_params=params(),
        cost_estimate=pl.CostEstimate(
            flops=pairs * leaf_size * leaf_size * 512,
            bytes_accessed=20 * vectors.size,
            transcendentals=pairs * leaf_size * leaf_size,
        ),
        name="near_field",
    )(
        near_slots,
        points_before,
        sites,
        points_after,
        vectors_before,
        vectors,
        vectors_after,
    )

    return pl.pallas_call(
        far_kernel,
        grid=(nparents,),
        out_shape=jax.ShapeDtypeStruct((ldev, count, leaf_size), f32),
        in_specs=[
            scalars(),
            scalars(),
            whole(coefs),
            whole(coefs),
            whole(coefs),
            whole(every),
            part(couplings, CHILDREN),
            part(coarse_couplings, 1),
            part(transfer, CHILDREN),
            part(basis, CHILDREN),
            part(near, CHILDREN),
        ],
        out_specs=pl.BlockSpec((CHILDREN, count, leaf_size), lambda i: (i, 0, 0)),
        scratch_shapes=[
            pltpu.VMEM((blank + 1, 2 * count, rank), bf16),
            pltpu.VMEM((every.shape[0] + 1, 2 * count, rank), bf16),
        ],
        compiler_params=params(),
        cost_estimate=pl.CostEstimate(
            flops=couplings.size * 64,
            bytes_accessed=8 * couplings.size,
            transcendentals=0,
        ),
        name="far_field",
    )(
        far_slots,
        coarse_slots,
        coefs_before,
        coefs,
        coefs_after,
        every,
        couplings,
        coarse_couplings,
        transfer,
        basis,
        near,
    )


def solution(mesh):
    three_d = P(AXES, None, None)
    placed = (
        three_d,
        P(AXES, None),
        three_d,
        three_d,
        three_d,
        P(AXES, None, None, None),
        P(AXES, None, None, None),
        P(AXES, None),
        P(AXES, None),
        P(AXES, None),
    )
    return jax.shard_map(
        on_device,
        mesh=mesh,
        in_specs=placed,
        out_specs=three_d,
        check_vma=False,
    )
```

```python
import functools
import math

import jax
import jax.numpy as jnp
from jax import lax
from jax.experimental import pallas as pl
from jax.experimental.pallas import tpu as pltpu
from jax.sharding import PartitionSpec as P

LEAF = 256
NEAR = 16
ELL2 = 0.25
AXES = ("leaf", "sub")
CHILDREN = 8
FEATURES = 32
VMEM_BYTES = 56 * 1024 * 1024
f32 = jnp.float32
bf16 = jnp.bfloat16


def three(x):
    high = x.astype(bf16).astype(f32)
    rest = x - high
    mid = rest.astype(bf16).astype(f32)
    return high, mid, rest - mid


def split(x):
    high = x.astype(bf16)
    return high, (x - high.astype(f32)).astype(bf16)


def stacked_rows(x):
    high = x.astype(bf16).astype(f32)
    return jnp.concatenate([high, x - high], axis=0).astype(bf16)


def dot(a, b):
    return jnp.dot(a, b, preferred_element_type=f32)


def dot_t(a, b):
    return lax.dot_general(a, b, (((1,), (1,)), ((), ())), preferred_element_type=f32)


def folded(x):
    half = x.shape[0] // 2
    return x[:half] + x[half:]


def packed(parent):
    half = parent.shape[0] // 2
    return jnp.concatenate([parent[:half], parent[half:]], axis=1)


def unpacked(half):
    rank = half.shape[1] // 2
    return jnp.concatenate([half[:, :rank], half[:, rank:]], axis=0)


def exchange_kernel(
    count,
    sites,
    vectors,
    basis,
    transfer,
    sites_before,
    sites_after,
    vectors_before,
    vectors_after,
    coefs,
    coefs_before,
    coefs_after,
    every,
    halo_send,
    halo_recv,
    all_send,
    all_recv,
):
    inner = lax.axis_size("sub")
    me = lax.axis_index("leaf") * inner + lax.axis_index("sub")
    pairs = every.shape[0] // count
    mine = every.at[pl.ds(me * pairs, pairs)]

    def device(step):
        to = lax.rem(me + step, count)
        return (to // inner, lax.rem(to, inner))

    barrier = pltpu.get_barrier_semaphore()

    def greet(step, carry):
        pl.semaphore_signal(
            barrier, inc=1, device_id=device(step), device_id_type=pl.DeviceIdType.MESH
        )
        return carry

    lax.fori_loop(1, count, greet, 0)
    pl.semaphore_wait(barrier, count - 1)

    def send(at, source, target, step):
        return pltpu.make_async_remote_copy(
            src_ref=source,
            dst_ref=target,
            send_sem=halo_send.at[at],
            recv_sem=halo_recv.at[at],
            device_id=device(step),
            device_id_type=pl.DeviceIdType.MESH,
        )

    right, left = 1, count - 1
    copies = [
        send(0, sites, sites_before, right),
        send(1, sites, sites_after, left),
        send(2, vectors, vectors_before, right),
        send(3, vectors, vectors_after, left),
    ]
    for copy in copies:
        copy.start()

    def upward(parent):
        total = jnp.zeros((16, transfer.shape[2]), f32)
        for q in range(CHILDREN):
            at = parent * CHILDREN + q
            high, low = split(basis[at])
            rows = stacked_rows(vectors[at])
            one = folded(dot_t(rows, high) + dot_t(rows, low))
            coefs[at] = one
            rows = stacked_rows(one)
            high, low = split(transfer[at])
            total = total + dot(rows, high) + dot(rows, low)
        return packed(folded(total))

    def pair(at, carry):
        every[me * pairs + at] = jnp.concatenate([upward(2 * at), upward(2 * at + 1)], axis=0)
        return carry

    lax.fori_loop(0, pairs, pair, 0)

    late = [send(4, coefs, coefs_before, right), send(5, coefs, coefs_after, left)]
    for copy in late:
        copy.start()

    def share(step):
        return pltpu.make_async_remote_copy(
            src_ref=mine,
            dst_ref=mine,
            send_sem=all_send.at[step - 1],
            recv_sem=all_recv.at[step - 1],
            device_id=device(step),
            device_id_type=pl.DeviceIdType.MESH,
        )

    def begin(step, carry):
        share(step).start()
        return carry

    def finish(step, carry):
        share(step).wait()
        return carry

    lax.fori_loop(1, count, begin, 0)
    for copy in copies + late:
        copy.wait()
    lax.fori_loop(1, count, finish, 0)


def pieces(points, at):
    scale = math.sqrt(math.log2(math.e) / ELL2)
    rows = [points[c, pl.ds(at, 1), :] for c in range(3)]
    x = jnp.concatenate(rows, axis=0) * scale
    norm = -0.5 * jnp.sum(x * x, axis=0, keepdims=True)
    ones = jnp.ones((3, x.shape[1]), f32)
    rest = jnp.zeros((FEATURES - 24, x.shape[1]), f32)
    return three(x), three(norm), ones, rest


def own_features(points, at):
    (h, m, l), norm, ones, rest = pieces(points, at)
    return jnp.concatenate([h, m, h, l, h, m, *norm, ones, rest], axis=0).astype(bf16)


def other_features(points, at):
    (h, m, l), norm, ones, rest = pieces(points, at)
    rows = jnp.concatenate([h, h, m, h, l, m, ones, *norm, rest], axis=0)
    return jnp.transpose(rows).astype(bf16)


def near_kernel(
    slots,
    points_before,
    points_own,
    points_after,
    vectors_before,
    vectors_own,
    vectors_after,
    out,
    others,
    values,
    filled,
):
    blank = others.shape[0] - 1
    base = pl.program_id(0) * CHILDREN
    ldev = blank // 3

    @pl.when(pl.program_id(0) == 0)
    def _():
        sides = (
            (points_before, vectors_before),
            (points_own, vectors_own),
            (points_after, vectors_after),
        )

        def prepare(at, carry):
            for side, (points, vectors) in enumerate(sides):
                where = side * ldev + at
                others[where] = other_features(points, at)
                values[where] = stacked_rows(vectors[at] * points[3, pl.ds(at, 1), :])
            return carry

        lax.fori_loop(0, ldev, prepare, 0)
        others[blank] = jnp.zeros(others.shape[1:], bf16)
        values[blank] = jnp.zeros(values.shape[1:], bf16)

    gain = 4.0 * (LEAF * NEAR) ** (-0.5)
    width = slots.shape[1]

    def leaf(q, carry):
        count = jnp.int32(0)
        for n in range(width):
            j = slots[base + q, n]
            filled[count] = j
            count = count + jnp.where(j < blank, 1, 0)
        for n in range(3):
            filled[count + n] = blank
        mine = own_features(points_own, base + q)

        def some(first, many, total):
            for u in range(many):
                j = filled[first + u]
                kern = jnp.exp2(dot(others[j], mine))
                high, low = split(kern)
                rows = values[j]
                total = total + dot(rows, high) + dot(rows, low)
            return total

        total = jnp.zeros((16, out.shape[2]), f32)
        eights = count // 8
        total = lax.fori_loop(0, eights, lambda g, t: some(8 * g, 8, t), total)
        pairs = (count - 8 * eights + 1) // 2
        for many in range(1, 5):
            trips = jnp.where(pairs == many, 1, 0)
            total = lax.fori_loop(
                0, trips, lambda g, t, many=many: some(8 * eights, 2 * many, t), total
            )
        out[q] = folded(total) * (gain * points_own[3, pl.ds(base + q, 1), :])
        return carry

    lax.fori_loop(0, CHILDREN, leaf, 0)


def coupled(index, slots, table, matrix):
    rank = table.shape[2]
    total = jnp.zeros((64, 4 * rank), f32)
    for g in range(slots.shape[1] // 4):
        rows = jnp.concatenate([table[slots[index, 4 * g + u]] for u in range(4)], axis=0)
        high, low = split(matrix(4 * g))
        total = total + dot_t(rows, high) + dot_t(rows, low)
    blocks = [total[16 * u : 16 * u + 16, rank * u : rank * u + rank] for u in range(4)]
    return folded(blocks[0] + blocks[1] + blocks[2] + blocks[3])


def far_kernel(
    far_slots,
    coarse_slots,
    coefs_before,
    coefs_own,
    coefs_after,
    every,
    couplings,
    coarse,
    transfer,
    basis,
    near,
    out,
    coefs,
    parents,
):
    rank = transfer.shape[2]
    step = pl.program_id(0)
    ldev = coefs_own.shape[0]

    @pl.when(step == 0)
    def _():
        def prepare(at, carry):
            coefs[at] = stacked_rows(coefs_before[at])
            coefs[ldev + at] = stacked_rows(coefs_own[at])
            coefs[2 * ldev + at] = stacked_rows(coefs_after[at])
            return carry

        def prepare_parent(at, carry):
            both = every[at]
            half = both.shape[0] // 2
            parents[2 * at] = stacked_rows(unpacked(both[:half]))
            parents[2 * at + 1] = stacked_rows(unpacked(both[half:]))
            return carry

        lax.fori_loop(0, ldev, prepare, 0, unroll=2)
        lax.fori_loop(0, every.shape[0], prepare_parent, 0, unroll=4)
        coefs[3 * ldev] = jnp.zeros(coefs.shape[1:], bf16)
        parents[2 * every.shape[0]] = jnp.zeros(parents.shape[1:], bf16)

    field = coupled(
        step, coarse_slots, parents, lambda k: coarse[0, k : k + 4].reshape(4 * rank, rank)
    )
    above = stacked_rows(field)

    def leaf(q, carry):
        field = coupled(
            step * CHILDREN + q,
            far_slots,
            coefs,
            lambda k: couplings[q, k : k + 4].reshape(4 * rank, rank),
        )
        high, low = split(transfer[q])
        field = field + folded(dot_t(above, high) + dot_t(above, low))
        rows = stacked_rows(field)
        high, low = split(basis[q])
        out[q] = near[q] + folded(dot(rows, high) + dot(rows, low))
        return carry

    lax.fori_loop(0, CHILDREN, leaf, 0)


def whole(x):
    return pl.BlockSpec(x.shape, lambda i: (0,) * x.ndim)


def part(x, rows):
    return pl.BlockSpec((rows,) + x.shape[1:], lambda i: (i,) + (0,) * (x.ndim - 1))


def scalars():
    return pl.BlockSpec(memory_space=pltpu.SMEM)


def params():
    return pltpu.CompilerParams(vmem_limit_bytes=VMEM_BYTES)


def on_device(
    points,
    amplitude,
    vectors,
    basis,
    transfer,
    couplings,
    coarse_couplings,
    near_list,
    far_list,
    coarse_list,
):
    ldev, _, leaf_size = points.shape
    rank = transfer.shape[2]
    count = vectors.shape[1]
    nparents = ldev // CHILDREN
    offset = lax.axis_index(AXES) * ldev - ldev
    blank = 3 * ldev

    basis = basis.swapaxes(1, 2)
    sites = jnp.concatenate([points.swapaxes(0, 1), amplitude[None]], axis=0)
    devices = lax.axis_size(AXES)
    results = (
        sites.shape,
        sites.shape,
        vectors.shape,
        vectors.shape,
        (ldev, count, rank),
        (ldev, count, rank),
        (ldev, count, rank),
        (devices * nparents // 2, count, 2 * rank),
    )
    (
        points_before,
        points_after,
        vectors_before,
        vectors_after,
        coefs,
        coefs_before,
        coefs_after,
        every,
    ) = pl.pallas_call(
        functools.partial(exchange_kernel, devices),
        out_shape=tuple(jax.ShapeDtypeStruct(shape, f32) for shape in results),
        in_specs=[pl.BlockSpec(memory_space=pltpu.VMEM)] * 4,
        out_specs=tuple(pl.BlockSpec(memory_space=pltpu.VMEM) for _ in results),
        scratch_shapes=[
            pltpu.SemaphoreType.DMA((6,)),
            pltpu.SemaphoreType.DMA((6,)),
            pltpu.SemaphoreType.DMA((devices - 1,)),
            pltpu.SemaphoreType.DMA((devices - 1,)),
        ],
        compiler_params=pltpu.CompilerParams(
            vmem_limit_bytes=VMEM_BYTES, collective_id=0, has_side_effects=True
        ),
        cost_estimate=pl.CostEstimate(
            flops=8 * ldev * leaf_size * rank * 16,
            bytes_accessed=12 * ldev * leaf_size * rank,
            transcendentals=0,
        ),
        name="upward_exchange",
    )(sites, vectors, basis, transfer)

    near_slots = jnp.where(near_list >= 0, near_list - offset, blank)
    far_slots = jnp.where(far_list >= 0, far_list - offset, blank)
    coarse_slots = jnp.where(coarse_list >= 0, coarse_list, 2 * every.shape[0])

    pairs = ldev * near_list.shape[1]
    near = pl.pallas_call(
        near_kernel,
        grid=(nparents,),
        out_shape=jax.ShapeDtypeStruct((ldev, count, leaf_size), f32),
        in_specs=[scalars()] + [whole(sites)] * 3 + [whole(vectors)] * 3,
        out_specs=pl.BlockSpec((CHILDREN, count, leaf_size), lambda i: (i, 0, 0)),
        scratch_shapes=[
            pltpu.VMEM((blank + 1, leaf_size, FEATURES), bf16),
            pltpu.VMEM((blank + 1, 2 * count, leaf_size), bf16),
            pltpu.SMEM((near_list.shape[1] + 8,), jnp.int32),
        ],
        compiler_params=params(),
        cost_estimate=pl.CostEstimate(
            flops=pairs * leaf_size * leaf_size * 512,
            bytes_accessed=20 * vectors.size,
            transcendentals=pairs * leaf_size * leaf_size,
        ),
        name="near_field",
    )(
        near_slots,
        points_before,
        sites,
        points_after,
        vectors_before,
        vectors,
        vectors_after,
    )

    return pl.pallas_call(
        far_kernel,
        grid=(nparents,),
        out_shape=jax.ShapeDtypeStruct((ldev, count, leaf_size), f32),
        in_specs=[
            scalars(),
            scalars(),
            whole(coefs),
            whole(coefs),
            whole(coefs),
            whole(every),
            part(couplings, CHILDREN),
            part(coarse_couplings, 1),
            part(transfer, CHILDREN),
            part(basis, CHILDREN),
            part(near, CHILDREN),
        ],
        out_specs=pl.BlockSpec((CHILDREN, count, leaf_size), lambda i: (i, 0, 0)),
        scratch_shapes=[
            pltpu.VMEM((blank + 1, 2 * count, rank), bf16),
            pltpu.VMEM((2 * every.shape[0] + 1, 2 * count, rank), bf16),
        ],
        compiler_params=params(),
        cost_estimate=pl.CostEstimate(
            flops=couplings.size * 64,
            bytes_accessed=8 * couplings.size,
            transcendentals=0,
        ),
        name="far_field",
    )(
        far_slots,
        coarse_slots,
        coefs_before,
        coefs,
        coefs_after,
        every,
        couplings,
        coarse_couplings,
        transfer,
        basis,
        near,
    )


def solution(mesh):
    three_d = P(AXES, None, None)
    placed = (
        three_d,
        P(AXES, None),
        three_d,
        three_d,
        three_d,
        P(AXES, None, None, None),
        P(AXES, None, None, None),
        P(AXES, None),
        P(AXES, None),
        P(AXES, None),
    )
    return jax.shard_map(
        on_device,
        mesh=mesh,
        in_specs=placed,
        out_specs=three_d,
        check_vma=False,
    )
```

```python
import functools
import math

import jax
import jax.numpy as jnp
from jax import lax
from jax.experimental import pallas as pl
from jax.experimental.pallas import tpu as pltpu
from jax.sharding import PartitionSpec as P

LEAF = 256
NEAR = 16
ELL2 = 0.25
AXES = ("leaf", "sub")
FAR_UNROLL = 2
PREPARE_UNROLL = 2
CHILDREN = 8
FEATURES = 32
VMEM_BYTES = 56 * 1024 * 1024
f32 = jnp.float32
bf16 = jnp.bfloat16


def three(x):
    high = x.astype(bf16).astype(f32)
    rest = x - high
    mid = rest.astype(bf16).astype(f32)
    return high, mid, rest - mid


def split(x):
    high = x.astype(bf16)
    return high, (x - high.astype(f32)).astype(bf16)


def stacked_rows(x):
    high = x.astype(bf16).astype(f32)
    return jnp.concatenate([high, x - high], axis=0).astype(bf16)


def dot(a, b):
    return jnp.dot(a, b, preferred_element_type=f32)


def dot_t(a, b):
    return lax.dot_general(a, b, (((1,), (1,)), ((), ())), preferred_element_type=f32)


def folded(x):
    half = x.shape[0] // 2
    return x[:half] + x[half:]


def packed(parent):
    half = parent.shape[0] // 2
    return jnp.concatenate([parent[:half], parent[half:]], axis=1)


def unpacked(half):
    rank = half.shape[1] // 2
    return jnp.concatenate([half[:, :rank], half[:, rank:]], axis=0)


def exchange_kernel(
    count,
    sites,
    vectors,
    basis,
    transfer,
    sites_before,
    sites_after,
    vectors_before,
    vectors_after,
    coefs,
    coefs_before,
    coefs_after,
    every,
    halo_send,
    halo_recv,
    all_send,
    all_recv,
):
    inner = lax.axis_size("sub")
    me = lax.axis_index("leaf") * inner + lax.axis_index("sub")
    pairs = every.shape[0] // count
    mine = every.at[pl.ds(me * pairs, pairs)]

    def device(step):
        to = lax.rem(me + step, count)
        return (to // inner, lax.rem(to, inner))

    barrier = pltpu.get_barrier_semaphore()

    def greet(step, carry):
        pl.semaphore_signal(
            barrier, inc=1, device_id=device(step), device_id_type=pl.DeviceIdType.MESH
        )
        return carry

    lax.fori_loop(1, count, greet, 0)
    pl.semaphore_wait(barrier, count - 1)

    def send(at, source, target, step):
        return pltpu.make_async_remote_copy(
            src_ref=source,
            dst_ref=target,
            send_sem=halo_send.at[at],
            recv_sem=halo_recv.at[at],
            device_id=device(step),
            device_id_type=pl.DeviceIdType.MESH,
        )

    right, left = 1, count - 1
    copies = [
        send(0, sites, sites_before, right),
        send(1, sites, sites_after, left),
        send(2, vectors, vectors_before, right),
        send(3, vectors, vectors_after, left),
    ]
    for copy in copies:
        copy.start()

    def upward(parent):
        total = jnp.zeros((16, transfer.shape[2]), f32)
        for q in range(CHILDREN):
            at = parent * CHILDREN + q
            high, low = split(basis[at])
            rows = stacked_rows(vectors[at])
            one = folded(dot_t(rows, high) + dot_t(rows, low))
            coefs[at] = one
            rows = stacked_rows(one)
            high, low = split(transfer[at])
            total = total + dot(rows, high) + dot(rows, low)
        return packed(folded(total))

    def pair(at, carry):
        every[me * pairs + at] = jnp.concatenate([upward(2 * at), upward(2 * at + 1)], axis=0)
        return carry

    lax.fori_loop(0, pairs, pair, 0)

    late = [send(4, coefs, coefs_before, right), send(5, coefs, coefs_after, left)]
    for copy in late:
        copy.start()

    def share(step):
        return pltpu.make_async_remote_copy(
            src_ref=mine,
            dst_ref=mine,
            send_sem=all_send.at[step - 1],
            recv_sem=all_recv.at[step - 1],
            device_id=device(step),
            device_id_type=pl.DeviceIdType.MESH,
        )

    def begin(step, carry):
        share(step).start()
        return carry

    def finish(step, carry):
        share(step).wait()
        return carry

    lax.fori_loop(1, count, begin, 0)
    for copy in copies + late:
        copy.wait()
    lax.fori_loop(1, count, finish, 0)


def pieces(points, at):
    scale = math.sqrt(math.log2(math.e) / ELL2)
    rows = [points[c, pl.ds(at, 1), :] for c in range(3)]
    x = jnp.concatenate(rows, axis=0) * scale
    norm = -0.5 * jnp.sum(x * x, axis=0, keepdims=True)
    ones = jnp.ones((3, x.shape[1]), f32)
    rest = jnp.zeros((FEATURES - 24, x.shape[1]), f32)
    return three(x), three(norm), ones, rest


def own_features(points, at):
    (h, m, l), norm, ones, rest = pieces(points, at)
    return jnp.concatenate([h, m, h, l, h, m, *norm, ones, rest], axis=0).astype(bf16)


def other_features(points, at):
    (h, m, l), norm, ones, rest = pieces(points, at)
    rows = jnp.concatenate([h, h, m, h, l, m, ones, *norm, rest], axis=0)
    return jnp.transpose(rows).astype(bf16)


def near_kernel(
    slots,
    points_before,
    points_own,
    points_after,
    vectors_before,
    vectors_own,
    vectors_after,
    out,
    others,
    values,
    filled,
):
    blank = others.shape[0] - 1
    base = pl.program_id(0) * CHILDREN
    ldev = blank // 3

    @pl.when(pl.program_id(0) == 0)
    def _():
        sides = (
            (points_before, vectors_before),
            (points_own, vectors_own),
            (points_after, vectors_after),
        )

        def prepare(at, carry):
            for side, (points, vectors) in enumerate(sides):
                where = side * ldev + at
                others[where] = other_features(points, at)
                values[where] = stacked_rows(vectors[at] * points[3, pl.ds(at, 1), :])
            return carry

        lax.fori_loop(0, ldev, prepare, 0, unroll=PREPARE_UNROLL)
        others[blank] = jnp.zeros(others.shape[1:], bf16)
        values[blank] = jnp.zeros(values.shape[1:], bf16)

    gain = 4.0 * (LEAF * NEAR) ** (-0.5)
    width = slots.shape[1]

    def leaf(q, carry):
        count = jnp.int32(0)
        for n in range(width):
            j = slots[base + q, n]
            filled[count] = j
            count = count + jnp.where(j < blank, 1, 0)
        for n in range(3):
            filled[count + n] = blank
        mine = own_features(points_own, base + q)

        def some(first, many, total):
            for u in range(many):
                j = filled[first + u]
                kern = jnp.exp2(dot(others[j], mine))
                high, low = split(kern)
                rows = values[j]
                total = total + dot(rows, high) + dot(rows, low)
            return total

        total = jnp.zeros((16, out.shape[2]), f32)
        eights = count // 8
        total = lax.fori_loop(0, eights, lambda g, t: some(8 * g, 8, t), total)
        pairs = (count - 8 * eights + 1) // 2
        for many in range(1, 5):
            trips = jnp.where(pairs == many, 1, 0)
            total = lax.fori_loop(
                0, trips, lambda g, t, many=many: some(8 * eights, 2 * many, t), total
            )
        out[q] = folded(total) * (gain * points_own[3, pl.ds(base + q, 1), :])
        return carry

    lax.fori_loop(0, CHILDREN, leaf, 0)


def coupled(index, slots, table, matrix):
    rank = table.shape[2]
    total = jnp.zeros((64, 4 * rank), f32)
    for g in range(0, slots.shape[1], 8):
        left, right = [], []
        for first in (g, g + 4):
            rows = jnp.concatenate([table[slots[index, first + u]] for u in range(4)], axis=0)
            left += [rows, rows]
            full = matrix(first)
            high = full.astype(bf16).astype(f32)
            right += [high, full - high]
        right = jnp.concatenate(right, axis=1).astype(bf16)
        total = total + dot_t(jnp.concatenate(left, axis=1), right)
    blocks = [total[16 * u : 16 * u + 16, rank * u : rank * u + rank] for u in range(4)]
    return folded(blocks[0] + blocks[1] + blocks[2] + blocks[3])


def far_kernel(
    far_slots,
    coarse_slots,
    coefs_before,
    coefs_own,
    coefs_after,
    every,
    couplings,
    coarse,
    transfer,
    basis,
    near,
    out,
    coefs,
    parents,
):
    rank = transfer.shape[2]
    step = pl.program_id(0)
    ldev = coefs_own.shape[0]

    @pl.when(step == 0)
    def _():
        def prepare(at, carry):
            coefs[at] = stacked_rows(coefs_before[at])
            coefs[ldev + at] = stacked_rows(coefs_own[at])
            coefs[2 * ldev + at] = stacked_rows(coefs_after[at])
            return carry

        def prepare_parent(at, carry):
            both = every[at]
            half = both.shape[0] // 2
            parents[2 * at] = stacked_rows(unpacked(both[:half]))
            parents[2 * at + 1] = stacked_rows(unpacked(both[half:]))
            return carry

        lax.fori_loop(0, ldev, prepare, 0, unroll=2)
        lax.fori_loop(0, every.shape[0], prepare_parent, 0, unroll=4)
        coefs[3 * ldev] = jnp.zeros(coefs.shape[1:], bf16)
        parents[2 * every.shape[0]] = jnp.zeros(parents.shape[1:], bf16)

    field = coupled(
        step, coarse_slots, parents, lambda k: coarse[0, k : k + 4].reshape(4 * rank, rank)
    )
    above = stacked_rows(field)

    def leaf(q, carry):
        field = coupled(
            step * CHILDREN + q,
            far_slots,
            coefs,
            lambda k: couplings[q, k : k + 4].reshape(4 * rank, rank),
        )
        high, low = split(transfer[q])
        field = field + folded(dot_t(above, high) + dot_t(above, low))
        rows = stacked_rows(field)
        high, low = split(basis[q])
        out[q] = near[q] + folded(dot(rows, high) + dot(rows, low))
        return carry

    lax.fori_loop(0, CHILDREN, leaf, 0, unroll=FAR_UNROLL)


def whole(x):
    return pl.BlockSpec(x.shape, lambda i: (0,) * x.ndim)


def part(x, rows):
    return pl.BlockSpec((rows,) + x.shape[1:], lambda i: (i,) + (0,) * (x.ndim - 1))


def scalars():
    return pl.BlockSpec(memory_space=pltpu.SMEM)


def params():
    return pltpu.CompilerParams(vmem_limit_bytes=VMEM_BYTES)


def on_device(
    points,
    amplitude,
    vectors,
    basis,
    transfer,
    couplings,
    coarse_couplings,
    near_list,
    far_list,
    coarse_list,
):
    ldev, _, leaf_size = points.shape
    rank = transfer.shape[2]
    count = vectors.shape[1]
    nparents = ldev // CHILDREN
    offset = lax.axis_index(AXES) * ldev - ldev
    blank = 3 * ldev

    basis = basis.swapaxes(1, 2)
    sites = jnp.concatenate([points.swapaxes(0, 1), amplitude[None]], axis=0)
    devices = lax.axis_size(AXES)
    results = (
        sites.shape,
        sites.shape,
        vectors.shape,
        vectors.shape,
        (ldev, count, rank),
        (ldev, count, rank),
        (ldev, count, rank),
        (devices * nparents // 2, count, 2 * rank),
    )
    (
        points_before,
        points_after,
        vectors_before,
        vectors_after,
        coefs,
        coefs_before,
        coefs_after,
        every,
    ) = pl.pallas_call(
        functools.partial(exchange_kernel, devices),
        out_shape=tuple(jax.ShapeDtypeStruct(shape, f32) for shape in results),
        in_specs=[pl.BlockSpec(memory_space=pltpu.VMEM)] * 4,
        out_specs=tuple(pl.BlockSpec(memory_space=pltpu.VMEM) for _ in results),
        scratch_shapes=[
            pltpu.SemaphoreType.DMA((6,)),
            pltpu.SemaphoreType.DMA((6,)),
            pltpu.SemaphoreType.DMA((devices - 1,)),
            pltpu.SemaphoreType.DMA((devices - 1,)),
        ],
        compiler_params=pltpu.CompilerParams(
            vmem_limit_bytes=VMEM_BYTES, collective_id=0, has_side_effects=True
        ),
        cost_estimate=pl.CostEstimate(
            flops=8 * ldev * leaf_size * rank * 16,
            bytes_accessed=12 * ldev * leaf_size * rank,
            transcendentals=0,
        ),
        name="upward_exchange",
    )(sites, vectors, basis, transfer)

    near_slots = jnp.where(near_list >= 0, near_list - offset, blank)
    far_slots = jnp.where(far_list >= 0, far_list - offset, blank)
    coarse_slots = jnp.where(coarse_list >= 0, coarse_list, 2 * every.shape[0])

    pairs = ldev * near_list.shape[1]
    near = pl.pallas_call(
        near_kernel,
        grid=(nparents,),
        out_shape=jax.ShapeDtypeStruct((ldev, count, leaf_size), f32),
        in_specs=[scalars()] + [whole(sites)] * 3 + [whole(vectors)] * 3,
        out_specs=pl.BlockSpec((CHILDREN, count, leaf_size), lambda i: (i, 0, 0)),
        scratch_shapes=[
            pltpu.VMEM((blank + 1, leaf_size, FEATURES), bf16),
            pltpu.VMEM((blank + 1, 2 * count, leaf_size), bf16),
            pltpu.SMEM((near_list.shape[1] + 8,), jnp.int32),
        ],
        compiler_params=params(),
        cost_estimate=pl.CostEstimate(
            flops=pairs * leaf_size * leaf_size * 512,
            bytes_accessed=20 * vectors.size,
            transcendentals=pairs * leaf_size * leaf_size,
        ),
        name="near_field",
    )(
        near_slots,
        points_before,
        sites,
        points_after,
        vectors_before,
        vectors,
        vectors_after,
    )

    return pl.pallas_call(
        far_kernel,
        grid=(nparents,),
        out_shape=jax.ShapeDtypeStruct((ldev, count, leaf_size), f32),
        in_specs=[
            scalars(),
            scalars(),
            whole(coefs),
            whole(coefs),
            whole(coefs),
            whole(every),
            part(couplings, CHILDREN),
            part(coarse_couplings, 1),
            part(transfer, CHILDREN),
            part(basis, CHILDREN),
            part(near, CHILDREN),
        ],
        out_specs=pl.BlockSpec((CHILDREN, count, leaf_size), lambda i: (i, 0, 0)),
        scratch_shapes=[
            pltpu.VMEM((blank + 1, 2 * count, rank), bf16),
            pltpu.VMEM((2 * every.shape[0] + 1, 2 * count, rank), bf16),
        ],
        compiler_params=params(),
        cost_estimate=pl.CostEstimate(
            flops=couplings.size * 64,
            bytes_accessed=8 * couplings.size,
            transcendentals=0,
        ),
        name="far_field",
    )(
        far_slots,
        coarse_slots,
        coefs_before,
        coefs,
        coefs_after,
        every,
        couplings,
        coarse_couplings,
        transfer,
        basis,
        near,
    )


def solution(mesh):
    three_d = P(AXES, None, None)
    placed = (
        three_d,
        P(AXES, None),
        three_d,
        three_d,
        three_d,
        P(AXES, None, None, None),
        P(AXES, None, None, None),
        P(AXES, None),
        P(AXES, None),
        P(AXES, None),
    )
    return jax.shard_map(
        on_device,
        mesh=mesh,
        in_specs=placed,
        out_specs=three_d,
        check_vma=False,
    )
```

```python
import functools
import math

import jax
import jax.numpy as jnp
from jax import lax
from jax.experimental import pallas as pl
from jax.experimental.pallas import tpu as pltpu
from jax.sharding import PartitionSpec as P

LEAF = 256
NEAR = 16
ELL2 = 0.25
AXES = ("leaf", "sub")
FAR_UNROLL = 2
PREPARE_UNROLL = 2
CHILDREN = 8
FEATURES = 32
VMEM_BYTES = 56 * 1024 * 1024
f32 = jnp.float32
bf16 = jnp.bfloat16


def three(x):
    high = x.astype(bf16).astype(f32)
    rest = x - high
    mid = rest.astype(bf16).astype(f32)
    return high, mid, rest - mid


def split(x):
    high = x.astype(bf16)
    return high, (x - high.astype(f32)).astype(bf16)


def stacked_rows(x):
    high = x.astype(bf16).astype(f32)
    return jnp.concatenate([high, x - high], axis=0).astype(bf16)


def dot(a, b):
    return jnp.dot(a, b, preferred_element_type=f32)


def dot_t(a, b):
    return lax.dot_general(a, b, (((1,), (1,)), ((), ())), preferred_element_type=f32)


def folded(x):
    half = x.shape[0] // 2
    return x[:half] + x[half:]


def packed(parent):
    half = parent.shape[0] // 2
    return jnp.concatenate([parent[:half], parent[half:]], axis=1)


def unpacked(half):
    rank = half.shape[1] // 2
    return jnp.concatenate([half[:, :rank], half[:, rank:]], axis=0)


def exchange_kernel(
    count,
    sites,
    vectors,
    basis,
    transfer,
    sites_before,
    sites_after,
    vectors_before,
    vectors_after,
    coefs,
    coefs_before,
    coefs_after,
    every,
    halo_send,
    halo_recv,
    all_send,
    all_recv,
):
    inner = lax.axis_size("sub")
    me = lax.axis_index("leaf") * inner + lax.axis_index("sub")
    pairs = every.shape[0] // count
    mine = every.at[pl.ds(me * pairs, pairs)]

    def device(step):
        to = lax.rem(me + step, count)
        return (to // inner, lax.rem(to, inner))

    barrier = pltpu.get_barrier_semaphore()

    def greet(step, carry):
        pl.semaphore_signal(
            barrier, inc=1, device_id=device(step), device_id_type=pl.DeviceIdType.MESH
        )
        return carry

    lax.fori_loop(1, count, greet, 0)
    pl.semaphore_wait(barrier, count - 1)

    def send(at, source, target, step):
        return pltpu.make_async_remote_copy(
            src_ref=source,
            dst_ref=target,
            send_sem=halo_send.at[at],
            recv_sem=halo_recv.at[at],
            device_id=device(step),
            device_id_type=pl.DeviceIdType.MESH,
        )

    right, left = 1, count - 1
    copies = [
        send(0, sites, sites_before, right),
        send(1, sites, sites_after, left),
        send(2, vectors, vectors_before, right),
        send(3, vectors, vectors_after, left),
    ]
    has_right, has_left = me < count - 1, me > 0

    def start(pair):
        @pl.when(has_right)
        def _():
            pair[0].start()

        @pl.when(has_left)
        def _():
            pair[1].start()

    def wait(pair):
        @pl.when(has_right)
        def _():
            pair[0].wait_send()
            pair[1].wait_recv()

        @pl.when(has_left)
        def _():
            pair[1].wait_send()
            pair[0].wait_recv()

    start(copies[:2])
    start(copies[2:])

    @pl.when(me == 0)
    def _():
        for ref in (sites_before, vectors_before, coefs_before):
            ref[...] = jnp.zeros(ref.shape, f32)

    @pl.when(me == count - 1)
    def _():
        for ref in (sites_after, vectors_after, coefs_after):
            ref[...] = jnp.zeros(ref.shape, f32)

    def upward(parent):
        total = jnp.zeros((16, transfer.shape[2]), f32)
        for q in range(CHILDREN):
            at = parent * CHILDREN + q
            high, low = split(basis[at])
            rows = stacked_rows(vectors[at])
            one = folded(dot_t(rows, high) + dot_t(rows, low))
            coefs[at] = one
            rows = stacked_rows(one)
            high, low = split(transfer[at])
            total = total + dot(rows, high) + dot(rows, low)
        return packed(folded(total))

    def pair(at, carry):
        every[me * pairs + at] = jnp.concatenate([upward(2 * at), upward(2 * at + 1)], axis=0)
        return carry

    lax.fori_loop(0, pairs, pair, 0)

    late = [send(4, coefs, coefs_before, right), send(5, coefs, coefs_after, left)]
    start(late)

    def share(step):
        return pltpu.make_async_remote_copy(
            src_ref=mine,
            dst_ref=mine,
            send_sem=all_send.at[step - 1],
            recv_sem=all_recv.at[step - 1],
            device_id=device(step),
            device_id_type=pl.DeviceIdType.MESH,
        )

    def begin(step, carry):
        share(step).start()
        return carry

    def finish(step, carry):
        share(step).wait()
        return carry

    lax.fori_loop(1, count, begin, 0)
    wait(copies[:2])
    wait(copies[2:])
    wait(late)
    lax.fori_loop(1, count, finish, 0)


def pieces(points, at):
    scale = math.sqrt(math.log2(math.e) / ELL2)
    rows = [points[c, pl.ds(at, 1), :] for c in range(3)]
    x = jnp.concatenate(rows, axis=0) * scale
    norm = -0.5 * jnp.sum(x * x, axis=0, keepdims=True)
    ones = jnp.ones((3, x.shape[1]), f32)
    rest = jnp.zeros((FEATURES - 24, x.shape[1]), f32)
    return three(x), three(norm), ones, rest


def own_features(points, at):
    (h, m, l), norm, ones, rest = pieces(points, at)
    return jnp.concatenate([h, m, h, l, h, m, *norm, ones, rest], axis=0).astype(bf16)


def other_features(points, at):
    (h, m, l), norm, ones, rest = pieces(points, at)
    rows = jnp.concatenate([h, h, m, h, l, m, ones, *norm, rest], axis=0)
    return jnp.transpose(rows).astype(bf16)


def near_kernel(
    slots,
    points_before,
    points_own,
    points_after,
    vectors_before,
    vectors_own,
    vectors_after,
    out,
    others,
    values,
    filled,
):
    blank = others.shape[0] - 1
    base = pl.program_id(0) * CHILDREN
    ldev = blank // 3

    @pl.when(pl.program_id(0) == 0)
    def _():
        sides = (
            (points_before, vectors_before),
            (points_own, vectors_own),
            (points_after, vectors_after),
        )

        def prepare(at, carry):
            for side, (points, vectors) in enumerate(sides):
                where = side * ldev + at
                others[where] = other_features(points, at)
                values[where] = stacked_rows(vectors[at] * points[3, pl.ds(at, 1), :])
            return carry

        lax.fori_loop(0, ldev, prepare, 0, unroll=PREPARE_UNROLL)
        others[blank] = jnp.zeros(others.shape[1:], bf16)
        values[blank] = jnp.zeros(values.shape[1:], bf16)

    gain = 4.0 * (LEAF * NEAR) ** (-0.5)
    width = slots.shape[1]

    def leaf(q, carry):
        count = jnp.int32(0)
        for n in range(width):
            j = slots[base + q, n]
            filled[count] = j
            count = count + jnp.where(j < blank, 1, 0)
        for n in range(3):
            filled[count + n] = blank
        mine = own_features(points_own, base + q)

        def some(first, many, total):
            for u in range(many):
                j = filled[first + u]
                kern = jnp.exp2(dot(others[j], mine))
                high, low = split(kern)
                rows = values[j]
                total = total + dot(rows, high) + dot(rows, low)
            return total

        total = jnp.zeros((16, out.shape[2]), f32)
        eights = count // 8
        total = lax.fori_loop(0, eights, lambda g, t: some(8 * g, 8, t), total)
        pairs = (count - 8 * eights + 1) // 2
        for many in range(1, 5):
            trips = jnp.where(pairs == many, 1, 0)
            total = lax.fori_loop(
                0, trips, lambda g, t, many=many: some(8 * eights, 2 * many, t), total
            )
        out[q] = folded(total) * (gain * points_own[3, pl.ds(base + q, 1), :])
        return carry

    lax.fori_loop(0, CHILDREN, leaf, 0)


def coupled(index, slots, table, matrix):
    rank = table.shape[2]
    total = jnp.zeros((64, 4 * rank), f32)
    for g in range(0, slots.shape[1], 8):
        left, right = [], []
        for first in (g, g + 4):
            rows = jnp.concatenate([table[slots[index, first + u]] for u in range(4)], axis=0)
            left += [rows, rows]
            full = matrix(first)
            high = full.astype(bf16).astype(f32)
            right += [high, full - high]
        right = jnp.concatenate(right, axis=1).astype(bf16)
        total = total + dot_t(jnp.concatenate(left, axis=1), right)
    blocks = [total[16 * u : 16 * u + 16, rank * u : rank * u + rank] for u in range(4)]
    return folded(blocks[0] + blocks[1] + blocks[2] + blocks[3])


def far_kernel(
    far_slots,
    coarse_slots,
    coefs_before,
    coefs_own,
    coefs_after,
    every,
    couplings,
    coarse,
    transfer,
    basis,
    near,
    out,
    coefs,
    parents,
):
    rank = transfer.shape[2]
    step = pl.program_id(0)
    ldev = coefs_own.shape[0]

    @pl.when(step == 0)
    def _():
        def prepare(at, carry):
            coefs[at] = stacked_rows(coefs_before[at])
            coefs[ldev + at] = stacked_rows(coefs_own[at])
            coefs[2 * ldev + at] = stacked_rows(coefs_after[at])
            return carry

        def prepare_parent(at, carry):
            both = every[at]
            half = both.shape[0] // 2
            parents[2 * at] = stacked_rows(unpacked(both[:half]))
            parents[2 * at + 1] = stacked_rows(unpacked(both[half:]))
            return carry

        lax.fori_loop(0, ldev, prepare, 0, unroll=2)
        lax.fori_loop(0, every.shape[0], prepare_parent, 0, unroll=4)
        coefs[3 * ldev] = jnp.zeros(coefs.shape[1:], bf16)
        parents[2 * every.shape[0]] = jnp.zeros(parents.shape[1:], bf16)

    field = coupled(
        step, coarse_slots, parents, lambda k: coarse[0, k : k + 4].reshape(4 * rank, rank)
    )
    above = stacked_rows(field)

    def leaf(q, carry):
        field = coupled(
            step * CHILDREN + q,
            far_slots,
            coefs,
            lambda k: couplings[q, k : k + 4].reshape(4 * rank, rank),
        )
        high, low = split(transfer[q])
        field = field + folded(dot_t(above, high) + dot_t(above, low))
        rows = stacked_rows(field)
        high, low = split(basis[q])
        out[q] = near[q] + folded(dot(rows, high) + dot(rows, low))
        return carry

    lax.fori_loop(0, CHILDREN, leaf, 0, unroll=FAR_UNROLL)


def whole(x):
    return pl.BlockSpec(x.shape, lambda i: (0,) * x.ndim)


def part(x, rows):
    return pl.BlockSpec((rows,) + x.shape[1:], lambda i: (i,) + (0,) * (x.ndim - 1))


def scalars():
    return pl.BlockSpec(memory_space=pltpu.SMEM)


def params():
    return pltpu.CompilerParams(vmem_limit_bytes=VMEM_BYTES)


def on_device(
    points,
    amplitude,
    vectors,
    basis,
    transfer,
    couplings,
    coarse_couplings,
    near_list,
    far_list,
    coarse_list,
):
    ldev, _, leaf_size = points.shape
    rank = transfer.shape[2]
    count = vectors.shape[1]
    nparents = ldev // CHILDREN
    offset = lax.axis_index(AXES) * ldev - ldev
    blank = 3 * ldev

    basis = basis.swapaxes(1, 2)
    sites = jnp.concatenate([points.swapaxes(0, 1), amplitude[None]], axis=0)
    devices = lax.axis_size(AXES)
    results = (
        sites.shape,
        sites.shape,
        vectors.shape,
        vectors.shape,
        (ldev, count, rank),
        (ldev, count, rank),
        (ldev, count, rank),
        (devices * nparents // 2, count, 2 * rank),
    )
    (
        points_before,
        points_after,
        vectors_before,
        vectors_after,
        coefs,
        coefs_before,
        coefs_after,
        every,
    ) = pl.pallas_call(
        functools.partial(exchange_kernel, devices),
        out_shape=tuple(jax.ShapeDtypeStruct(shape, f32) for shape in results),
        in_specs=[pl.BlockSpec(memory_space=pltpu.VMEM)] * 4,
        out_specs=tuple(pl.BlockSpec(memory_space=pltpu.VMEM) for _ in results),
        scratch_shapes=[
            pltpu.SemaphoreType.DMA((6,)),
            pltpu.SemaphoreType.DMA((6,)),
            pltpu.SemaphoreType.DMA((devices - 1,)),
            pltpu.SemaphoreType.DMA((devices - 1,)),
        ],
        compiler_params=pltpu.CompilerParams(
            vmem_limit_bytes=VMEM_BYTES, collective_id=0, has_side_effects=True
        ),
        cost_estimate=pl.CostEstimate(
            flops=8 * ldev * leaf_size * rank * 16,
            bytes_accessed=12 * ldev * leaf_size * rank,
            transcendentals=0,
        ),
        name="upward_exchange",
    )(sites, vectors, basis, transfer)

    near_slots = jnp.where(near_list >= 0, near_list - offset, blank)
    far_slots = jnp.where(far_list >= 0, far_list - offset, blank)
    coarse_slots = jnp.where(coarse_list >= 0, coarse_list, 2 * every.shape[0])

    pairs = ldev * near_list.shape[1]
    near = pl.pallas_call(
        near_kernel,
        grid=(nparents,),
        out_shape=jax.ShapeDtypeStruct((ldev, count, leaf_size), f32),
        in_specs=[scalars()] + [whole(sites)] * 3 + [whole(vectors)] * 3,
        out_specs=pl.BlockSpec((CHILDREN, count, leaf_size), lambda i: (i, 0, 0)),
        scratch_shapes=[
            pltpu.VMEM((blank + 1, leaf_size, FEATURES), bf16),
            pltpu.VMEM((blank + 1, 2 * count, leaf_size), bf16),
            pltpu.SMEM((near_list.shape[1] + 8,), jnp.int32),
        ],
        compiler_params=params(),
        cost_estimate=pl.CostEstimate(
            flops=pairs * leaf_size * leaf_size * 512,
            bytes_accessed=20 * vectors.size,
            transcendentals=pairs * leaf_size * leaf_size,
        ),
        name="near_field",
    )(
        near_slots,
        points_before,
        sites,
        points_after,
        vectors_before,
        vectors,
        vectors_after,
    )

    return pl.pallas_call(
        far_kernel,
        grid=(nparents,),
        out_shape=jax.ShapeDtypeStruct((ldev, count, leaf_size), f32),
        in_specs=[
            scalars(),
            scalars(),
            whole(coefs),
            whole(coefs),
            whole(coefs),
            whole(every),
            part(couplings, CHILDREN),
            part(coarse_couplings, 1),
            part(transfer, CHILDREN),
            part(basis, CHILDREN),
            part(near, CHILDREN),
        ],
        out_specs=pl.BlockSpec((CHILDREN, count, leaf_size), lambda i: (i, 0, 0)),
        scratch_shapes=[
            pltpu.VMEM((blank + 1, 2 * count, rank), bf16),
            pltpu.VMEM((2 * every.shape[0] + 1, 2 * count, rank), bf16),
        ],
        compiler_params=params(),
        cost_estimate=pl.CostEstimate(
            flops=couplings.size * 64,
            bytes_accessed=8 * couplings.size,
            transcendentals=0,
        ),
        name="far_field",
    )(
        far_slots,
        coarse_slots,
        coefs_before,
        coefs,
        coefs_after,
        every,
        couplings,
        coarse_couplings,
        transfer,
        basis,
        near,
    )


def solution(mesh):
    three_d = P(AXES, None, None)
    placed = (
        three_d,
        P(AXES, None),
        three_d,
        three_d,
        three_d,
        P(AXES, None, None, None),
        P(AXES, None, None, None),
        P(AXES, None),
        P(AXES, None),
        P(AXES, None),
    )
    return jax.shard_map(
        on_device,
        mesh=mesh,
        in_specs=placed,
        out_specs=three_d,
        check_vma=False,
    )
```
